512 devices in a mesh: slab: 16 (over z_hi, x, core), trace: 32 (over y, z_lo).
Axes of the slice: x: 4, y: 4, z: 16 (z_hi: 2, z_lo: 8; z = z_hi * 8 + z_lo), core: 2. Of those that a mesh axis runs over, the one named last changes fastest.
Arguments:
- incident: float32 [4, 3072, 128], P(None, 'trace'), may hold values from -6 to 6
- green_interior: bfloat16 [16, 2, 4608, 3072], P('slab', None, 'trace'), may hold values from -0.078125 to 0.078125
- green_next: bfloat16 [16, 2, 3072, 3072], P('slab', None, 'trace'), may hold values from -0.0625 to 0.0625
- sources: float32 [16, 4, 3072, 128], P('slab', None, 'trace'), may hold values from -3 to 3
Outputs:
- interior: float32 [16, 4, 4608, 128], P('slab', None, 'trace')
- traces: float32 [16, 4, 3072, 128], P('slab', None, 'trace')
The draws below stay inside these ranges and needn't reach their ends.
All inputs are finite; a program needn't handle non-finite values.
Results may differ from the reference program's by a relative error of at most 0.014.
Values may be sent and summed in bfloat16 or wider, within the bound.
No kernel may reach another device: no remote copies, remote signals or barrier semaphores. Data moves between devices by JAX's collectives and lax.ppermute only.
A program may use at most 64 MiB of HBM per device.

```python
import jax
import jax.numpy as jnp

TR = 3072
INTER = 4608
SRC = 64
FRONTS = 4
SLABS = 16
N_SLAB = 16


def shard_levels(stream_key, extent, cuts, smallest, largest):
    def one(axis_at, blocks):
        heights = jax.random.uniform(jax.random.fold_in(jax.random.fold_in(stream_key, 6), axis_at), (blocks,), jnp.float32, smallest / len(cuts), largest / len(cuts))
        return jnp.repeat(jnp.exp(heights), extent[axis_at] // blocks).reshape((-1,) + (1,) * (len(extent) - axis_at - 1))

    level = one(*cuts[0])
    for cut in cuts[1:]:
        level = level * one(*cut)
    return level


def noise(key, dims, scale, bound, shards=(), kind=jnp.bfloat16):
    factor_of = shard_levels(key, dims, shards, -0.22, 0.18) if shards else 1.0
    result = jax.random.normal(key, dims, jnp.float32) * scale * factor_of
    return jnp.minimum(jnp.maximum(result, -bound), bound).astype(kind)


def setup_inputs(seed: int = 0) -> dict:
    key_of = jax.random.split(jax.random.key(seed), 5)
    return {
        "incident": noise(key_of[0], (FRONTS, TR, 2 * SRC), 1.0, 6.0, ((1, 32),), jnp.float32),
        "green_interior": noise(key_of[1], (SLABS, 2, INTER, TR), (2 * TR) ** -0.5, 0.078125, ((0, 16), (2, 32))),
        "green_next": noise(key_of[2], (SLABS, 2, TR, TR), (5 * TR // 2) ** -0.5, 0.0625, ((0, 16), (2, 32))),
        "sources": noise(key_of[3], (SLABS, FRONTS, TR, 2 * SRC), 0.5, 3.0, ((0, 16), (2, 32)), jnp.float32),
    }


def complex_apply(halves, vectors, batches):
    row_count = halves.shape[1]
    inner_width = halves.shape[2]
    half_cols = vectors.shape[1] // (2 * batches)
    product = jnp.dot(halves.reshape(2 * row_count, inner_width), vectors, preferred_element_type=jnp.float32)
    product = product.reshape(2, row_count, batches, 2, half_cols)
    real_part = product[0, :, :, 0] - product[1, :, :, 1]
    imag_part = product[0, :, :, 1] + product[1, :, :, 0]
    return jnp.stack([real_part, imag_part], axis=2)


def to_fronts(product):
    row_count, batches, two_parts, half_cols = product.shape
    return jnp.transpose(product, (1, 0, 2, 3)).reshape(batches, row_count, two_parts * half_cols)


def reference(incident, green_interior, green_next, sources):
    current = jnp.transpose(incident, (1, 0, 2)).reshape(TR, FRONTS * 2 * SRC).astype(jnp.bfloat16)
    interiors = []
    outgoing = []
    for slab_index in range(N_SLAB):
        interiors.append(to_fronts(complex_apply(green_interior[slab_index], current, FRONTS)))
        leaving = to_fronts(complex_apply(green_next[slab_index], current, FRONTS)) + sources[slab_index]
        outgoing.append(leaving)
        current = jnp.transpose(leaving, (1, 0, 2)).reshape(TR, FRONTS * 2 * SRC).astype(jnp.bfloat16)
    return jnp.stack(interiors), jnp.stack(outgoing)
```

```python
import jax
import jax.numpy as jnp
from jax import lax
from jax.experimental import pallas as pl
from jax.experimental.pallas import tpu as pltpu
from jax.sharding import Mesh, PartitionSpec as P

NB = 4
NY = 4
NZ = 8
NS = 16
BF = jnp.bfloat16
F32 = jnp.float32


def block_of(shape):
    lane = lax.broadcasted_iota(jnp.int32, shape, len(shape) - 1)
    return (lane // 16) % 4


def roll_blocks(x, k):
    k = (16 * k) % 128
    return pltpu.roll(x, k, x.ndim - 1) if k else x


def turn(x):
    lane = lax.broadcasted_iota(jnp.int32, x.shape, x.ndim - 1)
    swapped = pltpu.roll(x, 64, x.ndim - 1)
    return jnp.where(lane < 64, -swapped, swapped)


def pack_kernel(src_ref, out_ref):
    blk = block_of(src_ref.shape[1:])
    for b in range(NB):
        total = jnp.zeros(src_ref.shape[1:], F32)
        for y in range(NY):
            total = jnp.where(blk == y, roll_blocks(src_ref[y].astype(F32), y - b), total)
        out_ref[b] = total.astype(out_ref.dtype)


def swap_blocks(x, dtype):
    n, rows, lanes = x.shape
    step = 96
    return pl.pallas_call(
        pack_kernel,
        grid=(rows // step,),
        in_specs=[pl.BlockSpec((n, step, lanes), lambda i: (0, i, 0))],
        out_specs=pl.BlockSpec((n, step, lanes), lambda i: (0, i, 0)),
        out_shape=jax.ShapeDtypeStruct(x.shape, dtype),
        name="swap_blocks",
    )(x)


def step_kernel(idx_ref, g_ref, op_ref, src_ref, out_ref, send_ref, acc0, acc1):
    q = pl.program_id(0)
    g = g_ref[...]
    rows = NY * op_ref.shape[2]
    width = op_ref.shape[3]
    blk = block_of((rows, 128))
    for part, acc in ((0, acc0), (1, acc1)):
        d = jnp.dot(op_ref[:, part].reshape(rows, width), g, preferred_element_type=F32)
        acc[...] = jnp.where(blk == q, d, acc[...])

    @pl.when(q == NY - 1)
    def _():
        d = acc0[...] + turn(acc1[...])
        d = d + roll_blocks(d, 1)
        d = d + roll_blocks(d, 2)
        n = rows // NY
        small = block_of((n, 128))
        total = jnp.zeros((n, 128), F32)
        for y in range(NY):
            total = jnp.where(small == y, roll_blocks(d[y * n : (y + 1) * n], y - 3), total)
        total = total + src_ref[0]
        out_ref[...] = total
        send_ref[...] = total.astype(BF)


def apply_next(index, g, op, src):
    n = op.shape[2]
    depth = g.shape[0]
    return pl.pallas_call(
        step_kernel,
        grid_spec=pltpu.PrefetchScalarGridSpec(
            num_scalar_prefetch=1,
            grid=(NY,),
            in_specs=[
                pl.BlockSpec((depth, 128), lambda q, i: (0, 0)),
                pl.BlockSpec((NY, 2, n, depth), lambda q, i: (0, 0, 0, q)),
                pl.BlockSpec((1, n, 128), lambda q, i: (i[0], 0, 0)),
            ],
            out_specs=[
                pl.BlockSpec((n, 128), lambda q, i: (0, 0)),
                pl.BlockSpec((n, 128), lambda q, i: (0, 0)),
            ],
            scratch_shapes=[pltpu.VMEM((NY * n, 128), F32), pltpu.VMEM((NY * n, 128), F32)],
        ),
        out_shape=[jax.ShapeDtypeStruct((n, 128), F32), jax.ShapeDtypeStruct((n, 128), BF)],
        compiler_params=pltpu.CompilerParams(vmem_limit_bytes=24 * 2**20),
        cost_estimate=pl.CostEstimate(flops=2 * 8 * n * depth * 4 * 128, bytes_accessed=op.size * 2, transcendentals=0),
        name="apply_next",
    )(index, g, op, src)


def interior_kernel(op_ref, v_ref, out_ref):
    v = v_ref[0]
    d0 = jnp.dot(op_ref[0], v, preferred_element_type=F32)
    d1 = jnp.dot(op_ref[1], v, preferred_element_type=F32)
    out_ref[0] = d0 + turn(d1)


def apply_interior(op, v):
    _, n, depth = op.shape
    return pl.pallas_call(
        interior_kernel,
        grid=(NY,),
        in_specs=[
            pl.BlockSpec((2, n, depth), lambda f: (0, 0, 0)),
            pl.BlockSpec((1, depth, 128), lambda f: (f, 0, 0)),
        ],
        out_specs=pl.BlockSpec((1, n, 128), lambda f: (f, 0, 0)),
        out_shape=jax.ShapeDtypeStruct((NY, n, 128), F32),
        compiler_params=pltpu.CompilerParams(vmem_limit_bytes=24 * 2**20),
        name="apply_interior",
    )(op, v)


def spread(x, axis):
    copies = jnp.broadcast_to(x, (lax.axis_size(axis), *x.shape))
    return lax.all_to_all(copies, axis, split_axis=0, concat_axis=0, tiled=True)


def local(incident, green_interior, green_next, sources):
    s = lax.axis_index("slab")
    rows = incident.shape[1]
    op = spread(green_next[0], "y")
    inc = lax.all_to_all(incident.astype(BF), "y", 0, 0, tiled=True)
    src = lax.all_to_all(sources[0], "y", 0, 0, tiled=True)
    inc = swap_blocks(inc, BF)
    src = swap_blocks(src, F32)
    stored = jnp.zeros((NB + 2, NZ * rows, 128), BF)
    kept = jnp.zeros((NB + 2, rows, 128), F32)
    received = jnp.zeros((rows, 128), BF)
    for c in range(NS + NB - 1):
        entering = jnp.where(s == 0, inc[min(c, NB - 1)], received)
        g = spread(entering, "zl").reshape(NZ * rows, 128)
        batch = c - s
        chosen = jnp.clip(batch, 0, NB - 1).astype(jnp.int32).reshape(1)
        leaving, send = apply_next(chosen, g, op, src)
        if c < NS + NB - 2:
            pairs = [(a, a + 1) for a in range(NS - 1) if 0 <= c - a < NB]
            received = lax.ppermute(send, "slab", pairs)
        slot = jnp.clip(batch + 1, 0, NB + 1)
        stored = lax.dynamic_update_index_in_dim(stored, g, slot, 0)
        kept = lax.dynamic_update_index_in_dim(kept, leaving, slot, 0)
    traces = swap_blocks(kept[1 : NB + 1], F32)
    traces = lax.all_to_all(traces, "y", 0, 0, tiled=True)
    v = swap_blocks(stored[1 : NB + 1], BF).reshape(NY * NZ * rows, 128)
    fronts = spread(v, "y")
    interior = apply_interior(green_interior[0], fronts)
    return interior[None], traces[None]


def solution(mesh):
    fine = Mesh(mesh.devices.reshape(NS, NY, NZ), ("slab", "y", "zl"))
    trace = ("y", "zl")
    return jax.shard_map(
        local,
        mesh=fine,
        in_specs=(
            P(None, trace, None),
            P("slab", None, trace, None),
            P("slab", None, trace, None),
            P("slab", None, trace, None),
        ),
        out_specs=(P("slab", None, trace, None), P("slab", None, trace, None)),
        check_vma=False,
    )
```

```python
import jax
import jax.numpy as jnp
from jax import lax
from jax.experimental import pallas as pl
from jax.experimental.pallas import tpu as pltpu
from jax.sharding import Mesh, PartitionSpec as P

NB = 2
NY = 4
NH = 2
NZ = 4
NS = 16
BF = jnp.bfloat16
F32 = jnp.float32


def block_of(shape):
    lane = lax.broadcasted_iota(jnp.int32, shape, len(shape) - 1)
    return (lane // 16) % 4


def roll_blocks(x, k):
    k = (16 * k) % 128
    return pltpu.roll(x, k, x.ndim - 1) if k else x


def turn(x):
    lane = lax.broadcasted_iota(jnp.int32, x.shape, x.ndim - 1)
    swapped = pltpu.roll(x, 64, x.ndim - 1)
    return jnp.where(lane < 64, -swapped, swapped)


def pack_kernel(src_ref, out_ref):
    blk = block_of(src_ref.shape[1:])
    for b in range(NY):
        total = jnp.zeros(src_ref.shape[1:], F32)
        for y in range(NY):
            total = jnp.where(blk == y, roll_blocks(src_ref[y].astype(F32), y - b), total)
        out_ref[b] = total.astype(out_ref.dtype)


def swap_blocks(x, dtype, source=lambda i: i):
    n, rows, lanes = x.shape
    step = 96
    return pl.pallas_call(
        pack_kernel,
        grid=(rows // step,),
        in_specs=[pl.BlockSpec((n, step, lanes), lambda i: (0, source(i), 0))],
        out_specs=pl.BlockSpec((n, step, lanes), lambda i: (0, i, 0)),
        out_shape=jax.ShapeDtypeStruct(x.shape, dtype),
        name="swap_blocks",
    )(x)


def step_kernel(idx_ref, g_ref, near_ref, far_ref, src_ref, out_ref, send_ref):
    batch, half = idx_ref[0], idx_ref[1]
    n, depth = near_ref.shape[2], near_ref.shape[3] // NY
    rows = NY * n
    g = jnp.concatenate([g_ref[z, h] for h in range(NH) for z in range(NZ)], axis=0)
    blk = block_of((rows, 128))
    small = block_of((n, 128))
    for op_ref, h in ((near_ref, half), (far_ref, 1 - half)):
        parts = []
        for part in range(2):
            acc = jnp.zeros((rows, 128), F32)
            for q in range(NY):
                op = op_ref[:, part, :, depth * q : depth * (q + 1)].reshape(rows, depth)
                acc = jnp.where(blk == q, jnp.dot(op, g, preferred_element_type=F32), acc)
            parts.append(acc)
        d = parts[0] + turn(parts[1])
        d = d + roll_blocks(d, 1)
        d = d + roll_blocks(d, 2)
        total = jnp.zeros((n, 128), F32)
        for y in range(NY):
            total = jnp.where(small == y, roll_blocks(d[y * n : (y + 1) * n], y - 3), total)
        total = total + src_ref[h, batch]
        out_ref[h] = total
        send_ref[h] = total.astype(BF)


def apply_next(index, g, near, far, src):
    n, depth = near.shape[2], near.shape[3]
    whole = pl.BlockSpec(memory_space=pltpu.VMEM)
    return pl.pallas_call(
        step_kernel,
        in_specs=[pl.BlockSpec(memory_space=pltpu.SMEM), whole, whole, whole, whole],
        out_specs=[whole, whole],
        out_shape=[jax.ShapeDtypeStruct((NH, n, 128), F32), jax.ShapeDtypeStruct((NH, n, 128), BF)],
        compiler_params=pltpu.CompilerParams(vmem_limit_bytes=24 * 2**20),
        cost_estimate=pl.CostEstimate(flops=4 * 2 * NH * NY * n * depth * 128, bytes_accessed=near.size * 4, transcendentals=0),
        name="apply_next",
    )(index, g, near, far, src)


def interior_kernel(op_ref, v_ref, out_ref):
    v = v_ref[0]
    d0 = jnp.dot(op_ref[0], v, preferred_element_type=F32)
    d1 = jnp.dot(op_ref[1], v, preferred_element_type=F32)
    out_ref[0] = d0 + turn(d1)


def apply_interior(op, v):
    _, n, depth = op.shape
    return pl.pallas_call(
        interior_kernel,
        grid=(NY,),
        in_specs=[
            pl.BlockSpec((2, n, depth), lambda f: (0, 0, 0)),
            pl.BlockSpec((1, depth, 128), lambda f: (f, 0, 0)),
        ],
        out_specs=pl.BlockSpec((1, n, 128), lambda f: (f, 0, 0)),
        out_shape=jax.ShapeDtypeStruct((NY, n, 128), F32),
        compiler_params=pltpu.CompilerParams(vmem_limit_bytes=24 * 2**20),
        name="apply_interior",
    )(op, v)


def spread(x, axis):
    copies = jnp.broadcast_to(x, (lax.axis_size(axis), *x.shape))
    return lax.all_to_all(copies, axis, split_axis=0, concat_axis=0, tiled=True)


def local(incident, green_interior, green_next, sources):
    s = lax.axis_index("slab")
    half = lax.axis_index("zh")
    rows = incident.shape[1]
    op = green_next[0]
    far = lax.ppermute(op, "zh", [(0, 1), (1, 0)])
    inc = lax.all_to_all(incident.astype(BF), "y", 0, 0, tiled=True)
    src = lax.all_to_all(sources[0], "y", 0, 0, tiled=True)
    near = spread(op, "y")
    inc = swap_blocks(inc, BF).reshape(NH, NB, rows, 128)
    src = swap_blocks(src, F32).reshape(NH, NB, rows, 128)
    inc = lax.all_to_all(inc, "zh", 0, 0, tiled=True)
    src = lax.all_to_all(src, "zh", 0, 0, tiled=True)
    far = spread(far, "y")
    stored = jnp.zeros((NB + 2, NZ, NH, rows, 128), BF)
    kept = jnp.zeros((NB + 2, NH, rows, 128), F32)
    received = jnp.zeros((NH, rows, 128), BF)
    for c in range(NS + NB - 1):
        entering = jnp.where(s == 0, inc[:, min(c, NB - 1)], received)
        g = spread(entering, "zr")
        batch = c - s
        chosen = jnp.clip(batch, 0, NB - 1)
        index = jnp.stack([chosen, half]).astype(jnp.int32)
        leaving, send = apply_next(index, g, near, far, src)
        if c < NS + NB - 2:
            pairs = [(a, a + 1) for a in range(NS - 1) if 0 <= c - a < NB]
            received = lax.ppermute(send, "slab", pairs)
        slot = jnp.clip(batch + 1, 0, NB + 1)
        stored = lax.dynamic_update_index_in_dim(stored, g, slot, 0)
        kept = lax.dynamic_update_index_in_dim(kept, leaving, slot, 0)
    v = spread(stored[1 : NB + 1], "zh").reshape(NH * NB, NZ * NH * rows, 128)
    traces = lax.all_to_all(jnp.swapaxes(kept[1 : NB + 1], 0, 1), "zh", 0, 0, tiled=True)
    traces = swap_blocks(traces.reshape(NH * NB, rows, 128), F32)
    traces = lax.all_to_all(traces, "y", 0, 0, tiled=True)
    v = swap_blocks(v, BF, lambda i: (i % NZ) * NH + i // NZ).reshape(NY * NZ * NH * rows, 128)
    fronts = spread(v, "y")
    interior = apply_interior(green_interior[0], fronts)
    return interior[None], traces[None]


def solution(mesh):
    fine = Mesh(mesh.devices.reshape(NS, NY, NH, NZ), ("slab", "y", "zh", "zr"))
    trace = ("y", "zh", "zr")
    return jax.shard_map(
        local,
        mesh=fine,
        in_specs=(
            P(None, trace, None),
            P("slab", None, trace, None),
            P("slab", None, trace, None),
            P("slab", None, trace, None),
        ),
        out_specs=(P("slab", None, trace, None), P("slab", None, trace, None)),
        check_vma=False,
    )
```

```python
import jax
import jax.numpy as jnp
from jax import lax
from jax.experimental import pallas as pl
from jax.experimental.pallas import tpu as pltpu
from jax.sharding import Mesh, PartitionSpec as P

NB = 2
NY = 4
NH = 2
NZ = 4
NS = 16
BF = jnp.bfloat16
F32 = jnp.float32


def block_of(shape):
    lane = lax.broadcasted_iota(jnp.int32, shape, len(shape) - 1)
    return (lane // 16) % 4


def roll_blocks(x, k):
    k = (16 * k) % 128
    return pltpu.roll(x, k, x.ndim - 1) if k else x


def turn(x):
    lane = lax.broadcasted_iota(jnp.int32, x.shape, x.ndim - 1)
    swapped = pltpu.roll(x, 64, x.ndim - 1)
    return jnp.where(lane < 64, -swapped, swapped)


def pack_kernel(src_ref, out_ref):
    blk = block_of(src_ref.shape[1:])
    for b in range(NY):
        total = jnp.zeros(src_ref.shape[1:], F32)
        for y in range(NY):
            total = jnp.where(blk == y, roll_blocks(src_ref[y].astype(F32), y - b), total)
        out_ref[b] = total.astype(out_ref.dtype)


def swap_blocks(x, dtype):
    n, rows, lanes = x.shape
    step = 96
    return pl.pallas_call(
        pack_kernel,
        grid=(rows // step,),
        in_specs=[pl.BlockSpec((n, step, lanes), lambda i: (0, i, 0))],
        out_specs=pl.BlockSpec((n, step, lanes), lambda i: (0, i, 0)),
        out_shape=jax.ShapeDtypeStruct(x.shape, dtype),
        name="swap_blocks",
    )(x)


def step_kernel(idx_ref, g_ref, near_hbm, real_hbm, imag_a_hbm, imag_b_hbm, src_ref, out_ref, send_ref, op_ref, sems):
    batch, half = idx_ref[0], idx_ref[1]
    n, depth = op_ref.shape[2], op_ref.shape[3] // NY
    places = (
        (near_hbm.at[:, 0], op_ref.at[0]),
        (near_hbm.at[:, 1], op_ref.at[1]),
        (real_hbm, op_ref.at[2]),
        (imag_a_hbm, op_ref.at[3, :, : n // 2]),
        (imag_b_hbm, op_ref.at[3, :, n // 2 :]),
    )
    copies = [pltpu.make_async_copy(there, here, sems.at[k]) for k, (there, here) in enumerate(places)]
    for copy in copies:
        copy.start()
    rows = NY * n
    g = jnp.concatenate([g_ref[z, h] for h in range(NH) for z in range(NZ)], axis=0)
    blk = block_of((rows, 128))
    small = block_of((n, 128))
    for far, h in ((0, half), (1, 1 - half)):
        parts = []
        for part in range(2):
            acc = jnp.zeros((rows, 128), F32)
            copies[2 * far + part].wait()
            if far and part:
                copies[4].wait()
            for q in range(NY):
                op = op_ref[2 * far + part, :, :, depth * q : depth * (q + 1)].reshape(rows, depth)
                acc = jnp.where(blk == q, jnp.dot(op, g, preferred_element_type=F32), acc)
            parts.append(acc)
        d = parts[0] + turn(parts[1])
        d = d + roll_blocks(d, 1)
        d = d + roll_blocks(d, 2)
        total = jnp.zeros((n, 128), F32)
        for y in range(NY):
            total = jnp.where(small == y, roll_blocks(d[y * n : (y + 1) * n], y - 3), total)
        total = total + src_ref[h, batch]
        out_ref[h] = total
        send_ref[h] = total.astype(BF)


def apply_next(index, g, near, real, imag_a, imag_b, src):
    n, depth = real.shape[1], real.shape[2]
    there = pl.BlockSpec(memory_space=pl.ANY)
    whole = pl.BlockSpec(memory_space=pltpu.VMEM)
    return pl.pallas_call(
        step_kernel,
        in_specs=[pl.BlockSpec(memory_space=pltpu.SMEM), whole, there, there, there, there, whole],
        out_specs=[whole, whole],
        scratch_shapes=[pltpu.VMEM((4, NY, n, depth), BF), pltpu.SemaphoreType.DMA((5,))],
        out_shape=[jax.ShapeDtypeStruct((NH, n, 128), F32), jax.ShapeDtypeStruct((NH, n, 128), BF)],
        compiler_params=pltpu.CompilerParams(vmem_limit_bytes=24 * 2**20),
        cost_estimate=pl.CostEstimate(flops=4 * 2 * NH * NY * n * depth * 128, bytes_accessed=near.size * 4, transcendentals=0),
        name="apply_next",
    )(index, g, near, real, imag_a, imag_b, src)


def interior_kernel(half_ref, op_ref, sets_ref, last_ref, out_ref, v_ref):
    sets = [sets_ref.at[0, k] for k in range(2 * NB - 1)] + [last_ref.at[0]]
    first = half_ref[0] == 0
    n = last_ref.shape[3]
    blk = block_of((n, 128))
    for h in range(NH):
        for z in range(NZ):
            pieces = [r[z, h].astype(F32) for r in sets]
            low = [jnp.where(first, pieces[b], pieces[NB + b]) for b in range(NB)]
            high = [jnp.where(first, pieces[NB + b], pieces[b]) for b in range(NB)]
            for y in range(NY):
                total = jnp.zeros((n, 128), F32)
                for b, piece in enumerate(low + high):
                    total = jnp.where(blk == b, roll_blocks(piece, b - y), total)
                v_ref[((y * NH + h) * NZ + z) * n : ((y * NH + h) * NZ + z + 1) * n] = total.astype(BF)
    v = v_ref[...]
    d0 = jnp.dot(op_ref[0], v, preferred_element_type=F32)
    d1 = jnp.dot(op_ref[1], v, preferred_element_type=F32)
    out_ref[0] = d0 + turn(d1)


def apply_interior(half, op, sets, last):
    _, n, depth = op.shape
    spec_of = lambda x: pl.BlockSpec((1, *x.shape[1:]), lambda f: (f,) + (0,) * (x.ndim - 1))
    return pl.pallas_call(
        interior_kernel,
        grid=(NY,),
        in_specs=[pl.BlockSpec(memory_space=pltpu.SMEM), pl.BlockSpec((2, n, depth), lambda f: (0, 0, 0))]
        + [spec_of(sets), spec_of(last)],
        out_specs=pl.BlockSpec((1, n, 128), lambda f: (f, 0, 0)),
        out_shape=jax.ShapeDtypeStruct((NY, n, 128), F32),
        scratch_shapes=[pltpu.VMEM((depth, 128), BF)],
        compiler_params=pltpu.CompilerParams(vmem_limit_bytes=24 * 2**20),
        name="apply_interior",
    )(half, op, sets, last)


def spread(x, axis):
    copies = jnp.broadcast_to(x, (lax.axis_size(axis), *x.shape))
    return lax.all_to_all(copies, axis, split_axis=0, concat_axis=0, tiled=True)


def local(incident, green_interior, green_next, sources):
    s = lax.axis_index("slab")
    half = lax.axis_index("zh")
    rows = incident.shape[1]
    real, imag = green_next[0, 0], green_next[0, 1]
    imag_a, imag_b = imag[: rows // 2], imag[rows // 2 :]
    across = [(0, 1), (1, 0)]
    together = lax.optimization_barrier
    far_real = lax.ppermute(real, "zh", across)
    near = spread(green_next[0], "y")
    far_real, near, imag_a, imag_b, incident, sources = together((far_real, near, imag_a, imag_b, incident, sources))
    imag_a = lax.ppermute(imag_a, "zh", across)
    far_real = spread(far_real, "y")
    far_real, imag_a, imag_b, incident, sources = together((far_real, imag_a, imag_b, incident, sources))
    imag_b = lax.ppermute(imag_b, "zh", across)
    imag_a = spread(imag_a, "y")
    inc = lax.all_to_all(incident.astype(BF), "y", 0, 0, tiled=True)
    inc = swap_blocks(inc, BF).reshape(NH, NB, rows, 128)
    imag_a, imag_b, inc, sources = together((imag_a, imag_b, inc, sources))
    imag_b = spread(imag_b, "y")
    inc = lax.all_to_all(inc, "zh", 0, 0, tiled=True)
    src = lax.all_to_all(sources[0], "y", 0, 0, tiled=True)
    src = swap_blocks(src, F32).reshape(NH, NB, rows, 128)
    src = lax.all_to_all(src, "zh", 0, 0, tiled=True)
    stored = jnp.zeros((NB + 2, NZ, NH, rows, 128), BF)
    kept = jnp.zeros((NB + 2, NH, rows, 128), F32)
    received = jnp.zeros((NH, rows, 128), BF)
    for c in range(NS + NB - 1):
        entering = jnp.where(s == 0, inc[:, min(c, NB - 1)], received)
        g = spread(entering, "zr")
        if c == NS:
            g, far_first = together((g, far_first))
        batch = c - s
        chosen = jnp.clip(batch, 0, NB - 1)
        index = jnp.stack([chosen, half]).astype(jnp.int32)
        leaving, send = apply_next(index, g, near, far_real, imag_a, imag_b, src)
        if c < NS + NB - 2:
            pairs = [(a, a + 1) for a in range(NS - 1) if 0 <= c - a < NB]
            received = lax.ppermute(send, "slab", pairs)
        slot = jnp.clip(batch + 1, 0, NB + 1)
        stored = lax.dynamic_update_index_in_dim(stored, g, slot, 0)
        kept = lax.dynamic_update_index_in_dim(kept, leaving, slot, 0)
        if c == NS - 1:
            first = stored[1]
            far_first = lax.ppermute(first, "zh", across)
    second = stored[2]
    far_second = lax.ppermute(second, "zh", across)
    sets = spread(jnp.stack([first, second, far_first]), "y")
    traces = lax.all_to_all(jnp.swapaxes(kept[1 : NB + 1], 0, 1), "zh", 0, 0, tiled=True)
    far_second, sets, traces = together((far_second, sets, traces))
    far_second = spread(far_second, "y")
    traces = swap_blocks(traces.reshape(NH * NB, rows, 128), F32)
    traces = lax.all_to_all(traces, "y", 0, 0, tiled=True)
    interior = apply_interior(half.astype(jnp.int32).reshape(1), green_interior[0], sets, far_second)
    return interior[None], traces[None]


def solution(mesh):
    fine = Mesh(mesh.devices.reshape(NS, NY, NH, NZ), ("slab", "y", "zh", "zr"))
    trace = ("y", "zh", "zr")
    return jax.shard_map(
        local,
        mesh=fine,
        in_specs=(
            P(None, trace, None),
            P("slab", None, trace, None),
            P("slab", None, trace, None),
            P("slab", None, trace, None),
        ),
        out_specs=(P("slab", None, trace, None), P("slab", None, trace, None)),
        check_vma=False,
    )
```

```python
import jax
import jax.numpy as jnp
from jax import lax
from jax.experimental import pallas as pl
from jax.experimental.pallas import tpu as pltpu
from jax.sharding import Mesh, PartitionSpec as P

NB = 2
NY = 4
NH = 2
NZ = 4
NS = 16
BF = jnp.bfloat16
F32 = jnp.float32


def block_of(shape):
    lane = lax.broadcasted_iota(jnp.int32, shape, len(shape) - 1)
    return (lane // 16) % 4


def roll_blocks(x, k):
    k = (16 * k) % 128
    return pltpu.roll(x, k, x.ndim - 1) if k else x


def turn(x):
    lane = lax.broadcasted_iota(jnp.int32, x.shape, x.ndim - 1)
    swapped = pltpu.roll(x, 64, x.ndim - 1)
    return jnp.where(lane < 64, -swapped, swapped)


def pack_kernel(src_ref, out_ref):
    blk = block_of(src_ref.shape[1:])
    for b in range(NY):
        total = jnp.zeros(src_ref.shape[1:], F32)
        for y in range(NY):
            total = jnp.where(blk == y, roll_blocks(src_ref[y].astype(F32), y - b), total)
        out_ref[b] = total.astype(out_ref.dtype)


def swap_blocks(x, dtype):
    n, rows, lanes = x.shape
    step = 96
    return pl.pallas_call(
        pack_kernel,
        grid=(rows // step,),
        in_specs=[pl.BlockSpec((n, step, lanes), lambda i: (0, i, 0))],
        out_specs=pl.BlockSpec((n, step, lanes), lambda i: (0, i, 0)),
        out_shape=jax.ShapeDtypeStruct(x.shape, dtype),
        name="swap_blocks",
    )(x)


def step_kernel(idx_ref, g_ref, *refs):
    sources, (src_ref, out_ref, send_ref, op_ref, sems) = refs[:15], refs[15:]
    batch, half, y0 = idx_ref[0], idx_ref[1], idx_ref[2]
    n, depth = op_ref.shape[2], op_ref.shape[3] // NY
    whole, top, bottom = slice(0, n), slice(0, n // 2), slice(n // 2, n)
    own, up, down, two_real, two_imag = sources[:5]
    places = [
        [(own.at[p], 0, whole), (up.at[p], 3, whole), (down.at[p], 1, whole), (two, 2, whole)]
        for p, two in enumerate((two_real, two_imag))
    ] + [
        list(zip(sources[k : k + 5], (0, 3, 1, 2, 2), (whole, whole, whole, top, bottom))) for k in (5, 10)
    ]
    copies = [
        [
            pltpu.make_async_copy(there, op_ref.at[k, (y0 + step) % NY, part], sems.at[k, j])
            for j, (there, step, part) in enumerate(group)
        ]
        for k, group in enumerate(places)
    ]
    for copy in copies[0]:
        copy.start()
    rows = NY * n
    g = jnp.concatenate([g_ref[z, h] for h in range(NH) for z in range(NZ)], axis=0)
    blk = block_of((rows, 128))
    small = block_of((n, 128))
    for far, h in ((0, half), (1, 1 - half)):
        parts = []
        for part in range(2):
            acc = jnp.zeros((rows, 128), F32)
            k = 2 * far + part
            for copy in copies[k]:
                copy.wait()
            if k < 3:
                for copy in copies[k + 1]:
                    copy.start()
            for q in range(NY):
                op = op_ref[2 * far + part, :, :, depth * q : depth * (q + 1)].reshape(rows, depth)
                acc = jnp.where(blk == q, jnp.dot(op, g, preferred_element_type=F32), acc)
            parts.append(acc)
        d = parts[0] + turn(parts[1])
        d = d + roll_blocks(d, 1)
        d = d + roll_blocks(d, 2)
        total = jnp.zeros((n, 128), F32)
        for y in range(NY):
            total = jnp.where(small == y, roll_blocks(d[y * n : (y + 1) * n], y - 3), total)
        total = total + src_ref[h, batch]
        out_ref[h] = total
        send_ref[h] = total.astype(BF)


def apply_next(index, g, ops, src):
    n, depth = ops[5].shape
    there = pl.BlockSpec(memory_space=pl.ANY)
    whole = pl.BlockSpec(memory_space=pltpu.VMEM)
    return pl.pallas_call(
        step_kernel,
        in_specs=[pl.BlockSpec(memory_space=pltpu.SMEM), whole] + [there] * 15 + [whole],
        out_specs=[whole, whole],
        scratch_shapes=[pltpu.VMEM((4, NY, n, depth), BF), pltpu.SemaphoreType.DMA((4, 5))],
        out_shape=[jax.ShapeDtypeStruct((NH, n, 128), F32), jax.ShapeDtypeStruct((NH, n, 128), BF)],
        compiler_params=pltpu.CompilerParams(vmem_limit_bytes=24 * 2**20),
        cost_estimate=pl.CostEstimate(flops=4 * 2 * NH * NY * n * depth * 128, bytes_accessed=4 * NY * n * depth * 2, transcendentals=0),
        name="apply_next",
    )(index, g, *ops, src)


def interior_kernel(half_ref, op_ref, sets_ref, last_ref, out_ref, v_ref):
    sets = [sets_ref.at[0, k] for k in range(2 * NB - 1)] + [last_ref.at[0]]
    first = half_ref[0] == 0
    n = last_ref.shape[3]
    blk = block_of((n, 128))
    for h in range(NH):
        for z in range(NZ):
            pieces = [r[z, h].astype(F32) for r in sets]
            low = [jnp.where(first, pieces[b], pieces[NB + b]) for b in range(NB)]
            high = [jnp.where(first, pieces[NB + b], pieces[b]) for b in range(NB)]
            for y in range(NY):
                total = jnp.zeros((n, 128), F32)
                for b, piece in enumerate(low + high):
                    total = jnp.where(blk == b, roll_blocks(piece, b - y), total)
                v_ref[((y * NH + h) * NZ + z) * n : ((y * NH + h) * NZ + z + 1) * n] = total.astype(BF)
    v = v_ref[...]
    d0 = jnp.dot(op_ref[0], v, preferred_element_type=F32)
    d1 = jnp.dot(op_ref[1], v, preferred_element_type=F32)
    out_ref[0] = d0 + turn(d1)


def apply_interior(half, op, sets, last):
    _, n, depth = op.shape
    spec_of = lambda x: pl.BlockSpec((1, *x.shape[1:]), lambda f: (f,) + (0,) * (x.ndim - 1))
    return pl.pallas_call(
        interior_kernel,
        grid=(NY,),
        in_specs=[pl.BlockSpec(memory_space=pltpu.SMEM), pl.BlockSpec((2, n, depth), lambda f: (0, 0, 0))]
        + [spec_of(sets), spec_of(last)],
        out_specs=pl.BlockSpec((1, n, 128), lambda f: (f, 0, 0)),
        out_shape=jax.ShapeDtypeStruct((NY, n, 128), F32),
        scratch_shapes=[pltpu.VMEM((depth, 128), BF)],
        compiler_params=pltpu.CompilerParams(vmem_limit_bytes=24 * 2**20),
        name="apply_interior",
    )(half, op, sets, last)


def spread(x, axis):
    copies = jnp.broadcast_to(x, (lax.axis_size(axis), *x.shape))
    return lax.all_to_all(copies, axis, split_axis=0, concat_axis=0, tiled=True)


def ring(x, step):
    return lax.ppermute(x, "y", [(i, (i + step) % NY) for i in range(NY)])


def around(x):
    n = x.shape[0] // 2
    up, down = ring(x, 1), ring(x, -1)
    return [x, up, down, ring(up[:n], 1), ring(down[n:], -1)]


def local(incident, green_interior, green_next, sources):
    s = lax.axis_index("slab")
    half = lax.axis_index("zh")
    y = lax.axis_index("y")
    rows = incident.shape[1]
    op = green_next[0]
    across = [(0, 1), (1, 0)]
    together = lax.optimization_barrier
    far_real = lax.ppermute(op[0], "zh", across)
    up, down = ring(op, 1), ring(op, -1)
    two_real, two_imag = ring(up[0], 1), ring(down[1], -1)
    far_real, imag = together((far_real, op[1]))
    far_imag = lax.ppermute(imag, "zh", across)
    ops = [op, up, down, two_real, two_imag, *around(far_real), *around(far_imag)]
    inc = lax.all_to_all(incident.astype(BF), "y", 0, 0, tiled=True)
    inc = swap_blocks(inc, BF).reshape(NH, NB, rows, 128)
    inc = lax.all_to_all(inc, "zh", 0, 0, tiled=True)
    src = lax.all_to_all(sources[0], "y", 0, 0, tiled=True)
    src = swap_blocks(src, F32).reshape(NH, NB, rows, 128)
    src = lax.all_to_all(src, "zh", 0, 0, tiled=True)
    stored = jnp.zeros((NB + 2, NZ, NH, rows, 128), BF)
    kept = jnp.zeros((NB + 2, NH, rows, 128), F32)
    received = jnp.zeros((NH, rows, 128), BF)
    for c in range(NS + NB - 1):
        entering = jnp.where(s == 0, inc[:, min(c, NB - 1)], received)
        g = spread(entering, "zr")
        if c == NS:
            g, far_first = together((g, far_first))
        batch = c - s
        chosen = jnp.clip(batch, 0, NB - 1)
        index = jnp.stack([chosen, half, y]).astype(jnp.int32)
        leaving, send = apply_next(index, g, ops, src)
        if c < NS + NB - 2:
            pairs = [(a, a + 1) for a in range(NS - 1) if 0 <= c - a < NB]
            received = lax.ppermute(send, "slab", pairs)
        slot = jnp.clip(batch + 1, 0, NB + 1)
        stored = lax.dynamic_update_index_in_dim(stored, g, slot, 0)
        kept = lax.dynamic_update_index_in_dim(kept, leaving, slot, 0)
        if c == NS - 1:
            first = stored[1]
            far_first = lax.ppermute(first, "zh", across)
    second = stored[2]
    far_second = lax.ppermute(second, "zh", across)
    sets = spread(jnp.stack([first, second, far_first]), "y")
    traces = lax.all_to_all(jnp.swapaxes(kept[1 : NB + 1], 0, 1), "zh", 0, 0, tiled=True)
    far_second, sets, traces = together((far_second, sets, traces))
    far_second = spread(far_second, "y")
    traces = swap_blocks(traces.reshape(NH * NB, rows, 128), F32)
    traces = lax.all_to_all(traces, "y", 0, 0, tiled=True)
    interior = apply_interior(half.astype(jnp.int32).reshape(1), green_interior[0], sets, far_second)
    return interior[None], traces[None]


def solution(mesh):
    fine = Mesh(mesh.devices.reshape(NS, NY, NH, NZ), ("slab", "y", "zh", "zr"))
    trace = ("y", "zh", "zr")
    return jax.shard_map(
        local,
        mesh=fine,
        in_specs=(
            P(None, trace, None),
            P("slab", None, trace, None),
            P("slab", None, trace, None),
            P("slab", None, trace, None),
        ),
        out_specs=(P("slab", None, trace, None), P("slab", None, trace, None)),
        check_vma=False,
    )
```

```python
import jax
import jax.numpy as jnp
from jax import lax
from jax.experimental import pallas as pl
from jax.experimental.pallas import tpu as pltpu
from jax.sharding import Mesh, PartitionSpec as P

NB = 4
NY = 4
NZ = 8
NS = 16
BF = jnp.bfloat16
F32 = jnp.float32


def block_of(shape):
    lane = lax.broadcasted_iota(jnp.int32, shape, len(shape) - 1)
    return (lane // 16) % 4


def roll_blocks(x, k):
    k = (16 * k) % 128
    return pltpu.roll(x, k, x.ndim - 1) if k else x


def turn(x):
    lane = lax.broadcasted_iota(jnp.int32, x.shape, x.ndim - 1)
    swapped = pltpu.roll(x, 64, x.ndim - 1)
    return jnp.where(lane < 64, -swapped, swapped)


def pack_kernel(src_ref, out_ref):
    blk = block_of(src_ref.shape[1:])
    for b in range(NB):
        total = jnp.zeros(src_ref.shape[1:], F32)
        for y in range(NY):
            total = jnp.where(blk == y, roll_blocks(src_ref[y].astype(F32), y - b), total)
        out_ref[b] = total.astype(out_ref.dtype)


def swap_blocks(x, dtype):
    n, rows, lanes = x.shape
    step = 96
    return pl.pallas_call(
        pack_kernel,
        grid=(rows // step,),
        in_specs=[pl.BlockSpec((n, step, lanes), lambda i: (0, i, 0))],
        out_specs=pl.BlockSpec((n, step, lanes), lambda i: (0, i, 0)),
        out_shape=jax.ShapeDtypeStruct(x.shape, dtype),
        name="swap_blocks",
    )(x)


def step_kernel(idx_ref, g_ref, *refs):
    sources, (src_ref, out_ref, send_ref, op_ref, sems) = refs[:5], refs[5:]
    batch, y0 = idx_ref[0], idx_ref[1]
    n, depth = op_ref.shape[2], g_ref.shape[0]
    rows = NY * n
    own, up, down = sources[:3]
    copies = [
        [
            pltpu.make_async_copy(there, op_ref.at[p, (y0 + step) % NY], sems.at[p, j])
            for j, (there, step) in enumerate(((own.at[p], 0), (up.at[p], 3), (down.at[p], 1), (sources[3 + p], 2)))
        ]
        for p in range(2)
    ]
    for group in copies:
        for copy in group:
            copy.start()
    g = g_ref[...]
    blk = block_of((rows, 128))
    small = block_of((n, 128))
    parts = []
    for p in range(2):
        for copy in copies[p]:
            copy.wait()
        acc = jnp.zeros((rows, 128), F32)
        for q in range(NY):
            op = op_ref[p, :, :, depth * q : depth * (q + 1)].reshape(rows, depth)
            acc = jnp.where(blk == q, jnp.dot(op, g, preferred_element_type=F32), acc)
        parts.append(acc)
    d = parts[0] + turn(parts[1])
    d = d + roll_blocks(d, 1)
    d = d + roll_blocks(d, 2)
    total = jnp.zeros((n, 128), F32)
    for y in range(NY):
        total = jnp.where(small == y, roll_blocks(d[y * n : (y + 1) * n], y - 3), total)
    total = total + src_ref[batch]
    out_ref[...] = total
    send_ref[...] = total.astype(BF)


def apply_next(index, g, ops, src):
    n, depth = ops[3].shape
    there = pl.BlockSpec(memory_space=pl.ANY)
    whole = pl.BlockSpec(memory_space=pltpu.VMEM)
    return pl.pallas_call(
        step_kernel,
        in_specs=[pl.BlockSpec(memory_space=pltpu.SMEM), whole] + [there] * 5 + [whole],
        out_specs=[whole, whole],
        scratch_shapes=[pltpu.VMEM((2, NY, n, depth), BF), pltpu.SemaphoreType.DMA((2, NY))],
        out_shape=[jax.ShapeDtypeStruct((n, 128), F32), jax.ShapeDtypeStruct((n, 128), BF)],
        compiler_params=pltpu.CompilerParams(vmem_limit_bytes=24 * 2**20),
        cost_estimate=pl.CostEstimate(
            flops=4 * NY * n * depth * 128, bytes_accessed=4 * NY * n * depth, transcendentals=0
        ),
        name="apply_next",
    )(index, g, *ops, src)


def interior_kernel(idx_ref, op_ref, own_ref, up_ref, down_ref, top_ref, bottom_ref, last_ref, out_ref, v_ref):
    y0 = idx_ref[0]
    n = 96
    pieces = own_ref.shape[1] // n
    blk = block_of((n, 128))
    fronts = ((own_ref, 0), (up_ref, 3), (down_ref, 1), (None, 2))
    for ref, step in fronts:
        front = (y0 + step) % NY
        for z in range(pieces):
            at = slice(z * n, (z + 1) * n)
            if ref is not None:
                sets = [ref[b, at] for b in range(NB - 1)]
            elif z < pieces // 2:
                sets = [top_ref[b, at] for b in range(NB - 1)]
            else:
                sets = [bottom_ref[b, z * n - bottom_ref.shape[1] : (z + 1) * n - bottom_ref.shape[1]] for b in range(NB - 1)]
            sets = [x.astype(F32) for x in sets + [last_ref[front, at]]]
            for y in range(NY):
                total = jnp.zeros((n, 128), F32)
                for b, x in enumerate(sets):
                    total = jnp.where(blk == b, roll_blocks(x, b - y), total)
                v_ref[(y * pieces + z) * n : (y * pieces + z + 1) * n] = total.astype(BF)
        v = v_ref[...]
        d0 = jnp.dot(op_ref[0], v, preferred_element_type=F32)
        d1 = jnp.dot(op_ref[1], v, preferred_element_type=F32)
        out_ref[front] = d0 + turn(d1)


def apply_interior(index, op, sets):
    _, n, depth = op.shape
    whole = pl.BlockSpec(memory_space=pltpu.VMEM)
    return pl.pallas_call(
        interior_kernel,
        in_specs=[pl.BlockSpec(memory_space=pltpu.SMEM)] + [whole] * 7,
        out_specs=whole,
        out_shape=jax.ShapeDtypeStruct((NY, n, 128), F32),
        scratch_shapes=[pltpu.VMEM((depth, 128), BF)],
        compiler_params=pltpu.CompilerParams(vmem_limit_bytes=24 * 2**20),
        name="apply_interior",
    )(index, op, *sets)


def spread(x, axis):
    copies = jnp.broadcast_to(x, (lax.axis_size(axis), *x.shape))
    return lax.all_to_all(copies, axis, split_axis=0, concat_axis=0, tiled=True)


def ring(x, step):
    return lax.ppermute(x, "y", [(i, (i + step) % NY) for i in range(NY)])


def local(incident, green_interior, green_next, sources):
    s = lax.axis_index("slab")
    y = lax.axis_index("y")
    rows = incident.shape[1]
    together = lax.optimization_barrier
    op = green_next[0]
    up, down = ring(op, 1), ring(op, -1)
    ops = [op, up, down, ring(up[0], 1), ring(down[1], -1)]
    inc = lax.all_to_all(incident.astype(BF), "y", 0, 0, tiled=True)
    src = lax.all_to_all(sources[0], "y", 0, 0, tiled=True)
    inc = swap_blocks(inc, BF)
    src = swap_blocks(src, F32)
    stored = jnp.zeros((NB + 2, NZ * rows, 128), BF)
    kept = jnp.zeros((NB + 2, rows, 128), F32)
    received = jnp.zeros((rows, 128), BF)
    last_step = NS + NB - 2
    for c in range(last_step + 1):
        entering = jnp.where(s == 0, inc[min(c, NB - 1)], received)
        g = spread(entering, "zl").reshape(NZ * rows, 128)
        if c == last_step:
            g, up, down = together((g, up, down))
        batch = c - s
        index = jnp.stack([jnp.clip(batch, 0, NB - 1), y]).astype(jnp.int32)
        leaving, send = apply_next(index, g, ops, src)
        if c < last_step:
            pairs = [(a, a + 1) for a in range(NS - 1) if 0 <= c - a < NB]
            received = lax.ppermute(send, "slab", pairs)
        slot = jnp.clip(batch + 1, 0, NB + 1)
        stored = lax.dynamic_update_index_in_dim(stored, g, slot, 0)
        kept = lax.dynamic_update_index_in_dim(kept, leaving, slot, 0)
        if c == last_step - 1:
            early = stored[1:NB]
            up, down = ring(early, 1), ring(early, -1)
    half = NZ * rows // 2
    top, bottom = ring(up[:, :half], 1), ring(down[:, half:], -1)
    last = spread(stored[NB], "y")
    traces = swap_blocks(kept[1 : NB + 1], F32)
    traces = lax.all_to_all(traces, "y", 0, 0, tiled=True)
    sets = (early, up, down, top, bottom, last)
    interior = apply_interior(y.astype(jnp.int32).reshape(1), green_interior[0], sets)
    return interior[None], traces[None]


def solution(mesh):
    fine = Mesh(mesh.devices.reshape(NS, NY, NZ), ("slab", "y", "zl"))
    trace = ("y", "zl")
    return jax.shard_map(
        local,
        mesh=fine,
        in_specs=(
            P(None, trace, None),
            P("slab", None, trace, None),
            P("slab", None, trace, None),
            P("slab", None, trace, None),
        ),
        out_specs=(P("slab", None, trace, None), P("slab", None, trace, None)),
        check_vma=False,
    )
```

```python
import jax
import jax.numpy as jnp
from jax import lax
from jax.experimental import pallas as pl
from jax.experimental.pallas import tpu as pltpu
from jax.sharding import Mesh, PartitionSpec as P

NB = 4
NY = 4
NZ = 8
NS = 16
BF = jnp.bfloat16
F32 = jnp.float32


def block_of(shape):
    lane = lax.broadcasted_iota(jnp.int32, shape, len(shape) - 1)
    return (lane // 16) % 4


def roll_blocks(x, k):
    k = (16 * k) % 128
    return pltpu.roll(x, k, x.ndim - 1) if k else x


def turn(x):
    lane = lax.broadcasted_iota(jnp.int32, x.shape, x.ndim - 1)
    swapped = pltpu.roll(x, 64, x.ndim - 1)
    return jnp.where(lane < 64, -swapped, swapped)


def pack_kernel(src_ref, out_ref):
    blk = block_of(src_ref.shape[1:])
    for b in range(NB):
        total = jnp.zeros(src_ref.shape[1:], F32)
        for y in range(NY):
            total = jnp.where(blk == y, roll_blocks(src_ref[y].astype(F32), y - b), total)
        out_ref[b] = total.astype(out_ref.dtype)


def swap_blocks(x, dtype):
    n, rows, lanes = x.shape
    step = 96
    return pl.pallas_call(
        pack_kernel,
        grid=(rows // step,),
        in_specs=[pl.BlockSpec((n, step, lanes), lambda i: (0, i, 0))],
        out_specs=pl.BlockSpec((n, step, lanes), lambda i: (0, i, 0)),
        out_shape=jax.ShapeDtypeStruct(x.shape, dtype),
        name="swap_blocks",
    )(x)


def hold_kernel(idx_ref, own, up, down, two_real, two_imag, real_ref, imag_ref, sems):
    copies = []
    for p, (out_ref, two) in enumerate(((real_ref, two_real), (imag_ref, two_imag))):
        for j, (there, step) in enumerate(((own.at[p], 0), (up.at[p], 3), (down.at[p], 1), (two, 2))):
            copies.append(pltpu.make_async_copy(there, out_ref.at[(idx_ref[0] + step) % NY], sems.at[p, j]))
    for copy in copies:
        copy.start()
    for copy in copies:
        copy.wait()


def hold(index, *pieces):
    there = pl.BlockSpec(memory_space=pl.ANY)
    shape = (NY, *pieces[3].shape)
    return pl.pallas_call(
        hold_kernel,
        in_specs=[pl.BlockSpec(memory_space=pltpu.SMEM)] + [there] * 5,
        out_specs=[pl.BlockSpec(memory_space=pltpu.VMEM), there],
        out_shape=[pltpu.VMEM(shape, BF), jax.ShapeDtypeStruct(shape, BF)],
        scratch_shapes=[pltpu.SemaphoreType.DMA((2, NY))],
        compiler_params=pltpu.CompilerParams(vmem_limit_bytes=16 * 2**20),
        name="hold",
    )(index, *pieces)


def step_kernel(idx_ref, g_ref, held_ref, imag_ref, src_ref, _a, _b, send_ref, kept_ref, stored_ref, out_ref, sems):
    batch, slot = idx_ref[0], idx_ref[1]
    n, depth = held_ref.shape[1], g_ref.shape[0]
    rows = NY * n
    keep = pltpu.make_async_copy(g_ref, stored_ref.at[slot], sems.at[0])
    keep.start()
    g = g_ref[...]
    blk = block_of((rows, 128))
    small = block_of((n, 128))
    parts = []
    for ref in (held_ref, imag_ref):
        acc = jnp.zeros((rows, 128), F32)
        for q in range(NY):
            op = ref[:, :, depth * q : depth * (q + 1)].reshape(rows, depth)
            acc = jnp.where(blk == q, jnp.dot(op, g, preferred_element_type=F32), acc)
        parts.append(acc)
    d = parts[0] + turn(parts[1])
    d = d + roll_blocks(d, 1)
    d = d + roll_blocks(d, 2)
    total = jnp.zeros((n, 128), F32)
    for y in range(NY):
        total = jnp.where(small == y, roll_blocks(d[y * n : (y + 1) * n], y - 3), total)
    total = total + src_ref[batch]
    out_ref[...] = total
    send_ref[...] = total.astype(BF)
    note = pltpu.make_async_copy(out_ref, kept_ref.at[slot], sems.at[1])
    note.start()
    keep.wait()
    note.wait()


def apply_next(index, g, held, imag, src, kept, stored):
    _, n, depth = imag.shape
    there = pl.BlockSpec(memory_space=pl.ANY)
    whole = pl.BlockSpec(memory_space=pltpu.VMEM)
    return pl.pallas_call(
        step_kernel,
        in_specs=[pl.BlockSpec(memory_space=pltpu.SMEM)] + [whole] * 4 + [there] * 2,
        out_specs=[whole, there, there],
        scratch_shapes=[pltpu.VMEM((n, 128), F32), pltpu.SemaphoreType.DMA((2,))],
        out_shape=[
            jax.ShapeDtypeStruct((n, 128), BF),
            pltpu.HBM(kept.shape, F32),
            pltpu.HBM(stored.shape, BF),
        ],
        input_output_aliases={5: 1, 6: 2},
        compiler_params=pltpu.CompilerParams(vmem_limit_bytes=16 * 2**20),
        cost_estimate=pl.CostEstimate(
            flops=4 * NY * n * depth * 128, bytes_accessed=4 * NY * n * depth, transcendentals=0
        ),
        name="apply_next",
    )(index, g, held, imag, src, kept, stored)


def interior_kernel(idx_ref, op_ref, own_ref, up_ref, down_ref, top_ref, bottom_ref, last_ref, out_ref, v_ref):
    y0 = idx_ref[0]
    n = 96
    pieces = own_ref.shape[1] // n
    blk = block_of((n, 128))
    fronts = ((own_ref, 0), (up_ref, 3), (down_ref, 1), (None, 2))
    for ref, step in fronts:
        front = (y0 + step) % NY
        for z in range(pieces):
            at = slice(z * n, (z + 1) * n)
            if ref is not None:
                sets = [ref[b, at] for b in range(NB - 1)]
            elif z < pieces // 2:
                sets = [top_ref[b, at] for b in range(NB - 1)]
            else:
                sets = [bottom_ref[b, z * n - bottom_ref.shape[1] : (z + 1) * n - bottom_ref.shape[1]] for b in range(NB - 1)]
            sets = [x.astype(F32) for x in sets + [last_ref[front, at]]]
            for y in range(NY):
                total = jnp.zeros((n, 128), F32)
                for b, x in enumerate(sets):
                    total = jnp.where(blk == b, roll_blocks(x, b - y), total)
                v_ref[(y * pieces + z) * n : (y * pieces + z + 1) * n] = total.astype(BF)
        v = v_ref[...]
        d0 = jnp.dot(op_ref[0], v, preferred_element_type=F32)
        d1 = jnp.dot(op_ref[1], v, preferred_element_type=F32)
        out_ref[front] = d0 + turn(d1)


def apply_interior(index, op, sets):
    _, n, depth = op.shape
    whole = pl.BlockSpec(memory_space=pltpu.VMEM)
    return pl.pallas_call(
        interior_kernel,
        in_specs=[pl.BlockSpec(memory_space=pltpu.SMEM)] + [whole] * 7,
        out_specs=whole,
        out_shape=jax.ShapeDtypeStruct((NY, n, 128), F32),
        scratch_shapes=[pltpu.VMEM((depth, 128), BF)],
        compiler_params=pltpu.CompilerParams(vmem_limit_bytes=24 * 2**20),
        name="apply_interior",
    )(index, op, *sets)


def spread(x, axis):
    copies = jnp.broadcast_to(x, (lax.axis_size(axis), *x.shape))
    return lax.all_to_all(copies, axis, split_axis=0, concat_axis=0, tiled=True)


def ring(x, step):
    return lax.ppermute(x, "y", [(i, (i + step) % NY) for i in range(NY)])


def local(incident, green_interior, green_next, sources):
    s = lax.axis_index("slab")
    y = lax.axis_index("y")
    rows = incident.shape[1]
    together = lax.optimization_barrier
    op = green_next[0]
    up, down = ring(op, 1), ring(op, -1)
    two_real, two_imag = ring(up[0], 1), ring(down[1], -1)
    held, imag = hold(y.astype(jnp.int32).reshape(1), op, up, down, two_real, two_imag)
    inc = lax.all_to_all(incident.astype(BF), "y", 0, 0, tiled=True)
    src = lax.all_to_all(sources[0], "y", 0, 0, tiled=True)
    inc = swap_blocks(inc, BF)
    src = swap_blocks(src, F32)
    stored = jnp.zeros((NB + 2, NZ * rows, 128), BF)
    kept = jnp.zeros((NB + 2, rows, 128), F32)
    received = jnp.zeros((rows, 128), BF)
    last_step = NS + NB - 2
    for c in range(last_step + 1):
        entering = jnp.where(s == 0, inc[c], received) if c < NB else received
        g = spread(entering, "zl").reshape(NZ * rows, 128)
        if c == last_step:
            g, up, down = together((g, up, down))
        batch = c - s
        slot = jnp.clip(batch + 1, 0, NB + 1)
        index = jnp.stack([jnp.clip(batch, 0, NB - 1), slot]).astype(jnp.int32)
        send, kept, stored = apply_next(index, g, held, imag, src, kept, stored)
        if c < last_step:
            pairs = [(a, a + 1) for a in range(NS - 1) if 0 <= c - a < NB]
            received = lax.ppermute(send, "slab", pairs)
        if c == last_step - 1:
            early = stored[1:NB]
            up, down = ring(early, 1), ring(early, -1)
    half = NZ * rows // 2
    top, bottom = ring(up[:, :half], 1), ring(down[:, half:], -1)
    last = spread(stored[NB], "y")
    traces = swap_blocks(kept[1 : NB + 1], F32)
    traces = lax.all_to_all(traces, "y", 0, 0, tiled=True)
    sets = (early, up, down, top, bottom, last)
    interior = apply_interior(y.astype(jnp.int32).reshape(1), green_interior[0], sets)
    return interior[None], traces[None]


def solution(mesh):
    fine = Mesh(mesh.devices.reshape(NS, NY, NZ), ("slab", "y", "zl"))
    trace = ("y", "zl")
    return jax.shard_map(
        local,
        mesh=fine,
        in_specs=(
            P(None, trace, None),
            P("slab", None, trace, None),
            P("slab", None, trace, None),
            P("slab", None, trace, None),
        ),
        out_specs=(P("slab", None, trace, None), P("slab", None, trace, None)),
        check_vma=False,
    )
```

```python
import jax
import jax.numpy as jnp
from jax import lax
from jax.experimental import pallas as pl
from jax.experimental.pallas import tpu as pltpu
from jax.sharding import Mesh, PartitionSpec as P

NB = 4
NY = 4
NZ = 8
NS = 16
BF = jnp.bfloat16
F32 = jnp.float32


def block_of(shape):
    lane = lax.broadcasted_iota(jnp.int32, shape, len(shape) - 1)
    return (lane // 16) % 4


def roll_blocks(x, k):
    k = (16 * k) % 128
    return pltpu.roll(x, k, x.ndim - 1) if k else x


def turn(x):
    lane = lax.broadcasted_iota(jnp.int32, x.shape, x.ndim - 1)
    swapped = pltpu.roll(x, 64, x.ndim - 1)
    return jnp.where(lane < 64, -swapped, swapped)


def pack_kernel(src_ref, out_ref):
    blk = block_of(src_ref.shape[1:])
    for b in range(NB):
        total = jnp.zeros(src_ref.shape[1:], F32)
        for y in range(NY):
            total = jnp.where(blk == y, roll_blocks(src_ref[y].astype(F32), y - b), total)
        out_ref[b] = total.astype(out_ref.dtype)


def swap_blocks(x, dtype):
    n, rows, lanes = x.shape
    step = 96
    return pl.pallas_call(
        pack_kernel,
        grid=(rows // step,),
        in_specs=[pl.BlockSpec((n, step, lanes), lambda i: (0, i, 0))],
        out_specs=pl.BlockSpec((n, step, lanes), lambda i: (0, i, 0)),
        out_shape=jax.ShapeDtypeStruct(x.shape, dtype),
        name="swap_blocks",
    )(x)


def hold_kernel(idx_ref, own, up, down, two_real, two_imag, real_ref, imag_ref, sems):
    copies = []
    for p, (out_ref, two) in enumerate(((real_ref, two_real), (imag_ref, two_imag))):
        for j, (there, step) in enumerate(((own.at[p], 0), (up.at[p], 3), (down.at[p], 1), (two, 2))):
            copies.append(pltpu.make_async_copy(there, out_ref.at[(idx_ref[0] + step) % NY], sems.at[p, j]))
    for copy in copies:
        copy.start()
    for copy in copies:
        copy.wait()


def hold(index, *pieces):
    there = pl.BlockSpec(memory_space=pl.ANY)
    shape = (NY, *pieces[3].shape)
    return pl.pallas_call(
        hold_kernel,
        in_specs=[pl.BlockSpec(memory_space=pltpu.SMEM)] + [there] * 5,
        out_specs=[pl.BlockSpec(memory_space=pltpu.VMEM), there],
        out_shape=[pltpu.VMEM(shape, BF), jax.ShapeDtypeStruct(shape, BF)],
        scratch_shapes=[pltpu.SemaphoreType.DMA((2, NY))],
        compiler_params=pltpu.CompilerParams(vmem_limit_bytes=16 * 2**20),
        name="hold",
    )(index, *pieces)


def step_kernel(idx_ref, g_ref, held_ref, imag_ref, src_ref, _a, _b, send_ref, kept_ref, stored_ref, out_ref, sems):
    batch, slot = idx_ref[0], idx_ref[1]
    n, depth = held_ref.shape[1], g_ref.shape[0]
    rows = NY * n
    keep = pltpu.make_async_copy(g_ref, stored_ref.at[slot], sems.at[0])
    keep.start()
    g = g_ref[...]
    blk = block_of((rows, 128))
    small = block_of((n, 128))
    parts = []
    for ref in (held_ref, imag_ref):
        acc = jnp.zeros((rows, 128), F32)
        for q in range(NY):
            op = ref[:, :, depth * q : depth * (q + 1)].reshape(rows, depth)
            acc = jnp.where(blk == q, jnp.dot(op, g, preferred_element_type=F32), acc)
        parts.append(acc)
    d = parts[0] + turn(parts[1])
    d = d + roll_blocks(d, 1)
    d = d + roll_blocks(d, 2)
    total = jnp.zeros((n, 128), F32)
    for y in range(NY):
        total = jnp.where(small == y, roll_blocks(d[y * n : (y + 1) * n], y - 3), total)
    total = total + src_ref[batch]
    out_ref[...] = total
    send_ref[...] = total.astype(BF)
    note = pltpu.make_async_copy(out_ref, kept_ref.at[slot], sems.at[1])
    note.start()
    keep.wait()
    note.wait()


def apply_next(index, g, held, imag, src, kept, stored):
    _, n, depth = imag.shape
    there = pl.BlockSpec(memory_space=pl.ANY)
    whole = pl.BlockSpec(memory_space=pltpu.VMEM)
    return pl.pallas_call(
        step_kernel,
        in_specs=[pl.BlockSpec(memory_space=pltpu.SMEM)] + [whole] * 4 + [there] * 2,
        out_specs=[whole, there, there],
        scratch_shapes=[pltpu.VMEM((n, 128), F32), pltpu.SemaphoreType.DMA((2,))],
        out_shape=[
            jax.ShapeDtypeStruct((n, 128), BF),
            pltpu.HBM(kept.shape, F32),
            pltpu.HBM(stored.shape, BF),
        ],
        input_output_aliases={5: 1, 6: 2},
        compiler_params=pltpu.CompilerParams(vmem_limit_bytes=16 * 2**20),
        cost_estimate=pl.CostEstimate(
            flops=4 * NY * n * depth * 128, bytes_accessed=4 * NY * n * depth, transcendentals=0
        ),
        name="apply_next",
    )(index, g, held, imag, src, kept, stored)


def interior_kernel(idx_ref, op_ref, own_ref, up_ref, down_ref, top_ref, bottom_ref, last_ref, out_ref, v_ref):
    y0 = idx_ref[0]
    n = 96
    pieces = own_ref.shape[1] // n
    blk = block_of((n, 128))
    fronts = ((own_ref, 0), (up_ref, 3), (down_ref, 1), (None, 2))
    for ref, step in fronts:
        front = (y0 + step) % NY
        for z in range(pieces):
            at = slice(z * n, (z + 1) * n)
            if ref is not None:
                sets = [ref[b, at] for b in range(NB - 1)]
            elif z < pieces // 2:
                sets = [top_ref[b, at] for b in range(NB - 1)]
            else:
                sets = [bottom_ref[b, z * n - bottom_ref.shape[1] : (z + 1) * n - bottom_ref.shape[1]] for b in range(NB - 1)]
            sets = [x.astype(F32) for x in sets + [last_ref[front, at]]]
            for y in range(NY):
                total = jnp.zeros((n, 128), F32)
                for b, x in enumerate(sets):
                    total = jnp.where(blk == b, roll_blocks(x, b - y), total)
                v_ref[(y * pieces + z) * n : (y * pieces + z + 1) * n] = total.astype(BF)
        v = v_ref[...]
        d0 = jnp.dot(op_ref[0], v, preferred_element_type=F32)
        d1 = jnp.dot(op_ref[1], v, preferred_element_type=F32)
        out_ref[front] = d0 + turn(d1)


def apply_interior(index, op, sets):
    _, n, depth = op.shape
    whole = pl.BlockSpec(memory_space=pltpu.VMEM)
    return pl.pallas_call(
        interior_kernel,
        in_specs=[pl.BlockSpec(memory_space=pltpu.SMEM)] + [whole] * 7,
        out_specs=whole,
        out_shape=jax.ShapeDtypeStruct((NY, n, 128), F32),
        scratch_shapes=[pltpu.VMEM((depth, 128), BF)],
        compiler_params=pltpu.CompilerParams(vmem_limit_bytes=24 * 2**20),
        name="apply_interior",
    )(index, op, *sets)


def spread(x, axis):
    copies = jnp.broadcast_to(x, (lax.axis_size(axis), *x.shape))
    return lax.all_to_all(copies, axis, split_axis=0, concat_axis=0, tiled=True)


def ring(x, step):
    return lax.ppermute(x, "y", [(i, (i + step) % NY) for i in range(NY)])


def local(incident, green_interior, green_next, sources):
    s = lax.axis_index("slab")
    y = lax.axis_index("y")
    rows = incident.shape[1]
    together = lax.optimization_barrier
    op = green_next[0]
    up, down = ring(op, 1), ring(op, -1)
    inc = lax.all_to_all(incident.astype(BF), "y", 0, 0, tiled=True)
    inc = swap_blocks(inc, BF)
    up, down, inc, sources = together((up, down, inc, sources))
    two_real, two_imag = ring(up[0], 1), ring(down[1], -1)
    held, imag = hold(y.astype(jnp.int32).reshape(1), op, up, down, two_real, two_imag)
    src = lax.all_to_all(sources[0], "y", 0, 0, tiled=True)
    src = swap_blocks(src, F32)
    stored = jnp.zeros((NB + 2, NZ * rows, 128), BF)
    kept = jnp.zeros((NB + 2, rows, 128), F32)
    received = jnp.zeros((rows, 128), BF)
    last_step = NS + NB - 2
    for c in range(last_step + 1):
        entering = jnp.where(s == 0, inc[c], received) if c < NB else received
        g = spread(entering, "zl").reshape(NZ * rows, 128)
        if c == last_step:
            g, up, down = together((g, up, down))
        batch = c - s
        slot = jnp.clip(batch + 1, 0, NB + 1)
        index = jnp.stack([jnp.clip(batch, 0, NB - 1), slot]).astype(jnp.int32)
        send, kept, stored = apply_next(index, g, held, imag, src, kept, stored)
        if c < last_step:
            pairs = [(a, a + 1) for a in range(NS - 1) if 0 <= c - a < NB]
            received = lax.ppermute(send, "slab", pairs)
        if c == last_step - 1:
            early = stored[1:NB]
            up, down = ring(early, 1), ring(early, -1)
    half = NZ * rows // 2
    top, bottom = ring(up[:, :half], 1), ring(down[:, half:], -1)
    last = spread(stored[NB], "y")
    kept, last = together((kept, last))
    traces = swap_blocks(kept[1 : NB + 1], F32)
    traces = lax.all_to_all(traces, "y", 0, 0, tiled=True)
    sets = (early, up, down, top, bottom, last)
    interior = apply_interior(y.astype(jnp.int32).reshape(1), green_interior[0], sets)
    return interior[None], traces[None]


def solution(mesh):
    fine = Mesh(mesh.devices.reshape(NS, NY, NZ), ("slab", "y", "zl"))
    trace = ("y", "zl")
    return jax.shard_map(
        local,
        mesh=fine,
        in_specs=(
            P(None, trace, None),
            P("slab", None, trace, None),
            P("slab", None, trace, None),
            P("slab", None, trace, None),
        ),
        out_specs=(P("slab", None, trace, None), P("slab", None, trace, None)),
        check_vma=False,
    )
```
